32 devices in a mesh: row: 8 (over z, y), col: 4 (over x, core).
Axes of the slice: x: 2, y: 2, z: 4, core: 2. Of those that a mesh axis runs over, the one named last changes fastest.
Arguments:
- sim_window: bfloat16 [1536, 1536], P('row', 'col'), as said below
- sim_rest: bfloat16 [1536, 118464], P('row', 'col'), may hold values from -6 to 6
- joined_partner_pairs: int32 [192, 2], replicated, may hold values from 0 to 1535, as said below
- cluster_member_count: int32 [1536], replicated, may hold values from 1 to 64
Outputs:
- window_out: bfloat16 [1536, 1536], P('row', 'col')
- rest_out: bfloat16 [1536, 118464], P('row', 'col')
The draws below stay inside these ranges and needn't reach their ends.
Inputs may be any that keep to these rules, and one draw needn't show every extreme that they name: `joined_partner_pairs`: each row is (survivor, partner); no window item appears twice in the whole list. Each aligned block of 192 items holds exactly 24 partners. For any two aligned blocks (possibly the same), at most 3 pairs have their partner in the first and their survivor in the second, and some two blocks have exactly 3. Nearly symmetric: sim_window[i, j] is close to sim_window[j, i].
All inputs are finite; a program needn't handle non-finite values.
Results may differ from the reference program's by a relative error of at most 0.001.
Values may be sent and summed in bfloat16 or wider, within the bound.
A program may use at most 128 MiB of HBM per device.

```python
import jax
import jax.numpy as jnp
from jax import lax

WINDOW_PER_ROW = 192
PARTNERS_PER_ROW = 24
CAP = 3
M = 1536
PAIRS = 192
REST = 118464


def block_shuffle(subkey):
    return jax.random.permutation(subkey, WINDOW_PER_ROW)


def draw_joined_partner_pairs(key, part):
    block_total = M // WINDOW_PER_ROW
    subkeys = jax.random.split(key, 3)
    block_order = jax.random.permutation(subkeys[0], block_total)
    hot_blocks = block_order[:4]
    cold_blocks = block_order[4:]
    pair_ids = jnp.arange(PAIRS, dtype=jnp.int32)
    src_index = pair_ids // PARTNERS_PER_ROW
    slot_index = pair_ids % PARTNERS_PER_ROW
    half_width = PARTNERS_PER_ROW // 2
    hot_dst = hot_blocks[jnp.minimum(slot_index // CAP, 3)]
    cold_dst = cold_blocks[(src_index + slot_index - half_width) % (block_total - 4)]
    destination_block = jnp.where(slot_index < half_width, hot_dst, cold_dst)
    row_permutations = jax.vmap(block_shuffle)(jax.random.split(subkeys[1], block_total))
    vanishing_node = src_index * WINDOW_PER_ROW + row_permutations[src_index, slot_index]
    one_hot = (destination_block[:, None] == jnp.arange(block_total, dtype=jnp.int32)[None, :]).astype(jnp.int32)
    incoming_entry = jnp.sum((jnp.cumsum(one_hot, axis=0) - one_hot) * one_hot, axis=1)
    lasting_node = destination_block * WINDOW_PER_ROW + row_permutations[destination_block, PARTNERS_PER_ROW + incoming_entry]
    reorder_indices = jax.random.permutation(subkeys[2], PAIRS)
    return jnp.stack([lasting_node, vanishing_node], axis=1)[reorder_indices].astype(jnp.int32)


def draw_sim_window(key, part):
    base = jax.random.normal(key, (M, M), jnp.float32)
    symmetric = (base + base.T) * 0.70710678
    return symmetric.astype(jnp.bfloat16)


def with_ends(values, key, low, high):
    longest = values.shape.index(max(values.shape))
    spots = []
    for shift in (0, 1):
        where = [jax.random.randint(jax.random.fold_in(key, axis), (), 0, length) for axis, length in enumerate(values.shape)]
        where[longest] = (where[longest] + shift) % values.shape[longest]
        spots.append(tuple(where))
    return values.at[spots[0]].set(low).at[spots[1]].set(high)


def shard_levels(stream_key, dims, shards, least, top_value):
    level, own = 1.0, jax.random.fold_in(stream_key, 6)
    for dim, parts in shards:
        steps = jnp.exp(jax.random.uniform(jax.random.fold_in(own, dim), (parts,), jnp.float32, least / len(shards), top_value / len(shards)))
        level = level * jnp.repeat(steps, dims[dim] // parts).reshape([-1 if axis == dim else 1 for axis in range(len(dims))])
    return level


def gaussian(own_key, dims, scale, limit, cuts=(), held_as=jnp.bfloat16):
    array = jax.random.normal(own_key, dims, jnp.float32) * scale
    if len(cuts) > 0:
        array = shard_levels(own_key, dims, cuts, -0.22, 0.18) * array
    return jnp.clip(array, min=-limit, max=limit).astype(held_as)


def setup_inputs(seed: int = 0) -> dict:
    streams_of = jax.random.split(jax.random.key(seed), 5)
    sim_window = draw_sim_window(jax.random.fold_in(streams_of[4], 71), 0)
    sim_rest = gaussian(streams_of[1], (M, REST), 1.0, 6.0, ((0, 8), (1, 4)))
    joined_partner_pairs = draw_joined_partner_pairs(jax.random.fold_in(streams_of[4], 71), 0)
    cluster_member_count = with_ends(jax.random.randint(streams_of[3], (M,), 1, 65), jax.random.fold_in(streams_of[3], 1), 1, 64).astype(jnp.int32)
    return dict(sim_window=sim_window, sim_rest=sim_rest, joined_partner_pairs=joined_partner_pairs, cluster_member_count=cluster_member_count)


def merge_weights(joined_partner_pairs, cluster_member_count):
    lasting_node = joined_partner_pairs[:, 0]
    vanishing_node = joined_partner_pairs[:, 1]
    remaining_size = cluster_member_count[lasting_node].astype(jnp.float32)
    absorbed_size = cluster_member_count[vanishing_node].astype(jnp.float32)
    joined_cluster_size = remaining_size + absorbed_size
    item_grand_sum = cluster_member_count.shape[0]
    retained_entries = jnp.ones((item_grand_sum,), jnp.float32).at[lasting_node].set(remaining_size / joined_cluster_size).at[vanishing_node].set(0.0)
    selected_entries = jnp.zeros((item_grand_sum,), jnp.float32).at[lasting_node].set(absorbed_size / joined_cluster_size)
    donor_position = jnp.zeros((item_grand_sum,), jnp.int32).at[lasting_node].set(vanishing_node.astype(jnp.int32))
    return retained_entries, selected_entries, donor_position


def combine_rows(matrix, retained_entries, selected_entries, donor_position):
    row_total = matrix.shape[0]
    block_rows = 128
    starts = jnp.arange(row_total // block_rows, dtype=jnp.int32) * block_rows

    def one_block(offset):
        own_rows = lax.dynamic_slice_in_dim(matrix, offset, block_rows, 0).astype(jnp.float32)
        source_ids = lax.dynamic_slice_in_dim(donor_position, offset, block_rows, 0).astype(jnp.int32)
        partner_rows = matrix[source_ids].astype(jnp.float32)
        keep_block = lax.dynamic_slice_in_dim(retained_entries, offset, block_rows, 0)
        take_block = lax.dynamic_slice_in_dim(selected_entries, offset, block_rows, 0)
        return (keep_block[:, None] * own_rows + take_block[:, None] * partner_rows).astype(jnp.bfloat16)

    blocks_out = lax.map(one_block, starts)
    return blocks_out.reshape(row_total, matrix.shape[1])


def reference(sim_window, sim_rest, joined_partner_pairs, cluster_member_count):
    retained_entries, selected_entries, donor_position = merge_weights(joined_partner_pairs, cluster_member_count)
    mixed_window = combine_rows(sim_window, retained_entries, selected_entries, donor_position)
    rest_out = combine_rows(sim_rest, retained_entries, selected_entries, donor_position)
    window_out = combine_rows(mixed_window.T, retained_entries, selected_entries, donor_position).T
    return window_out, rest_out
```

```python
import functools

import jax
import jax.numpy as jnp
from jax import lax
from jax.experimental import pallas as pl
from jax.experimental.pallas import tpu as pltpu
from jax.sharding import PartitionSpec as P

LANES = 128
GROUP = 8
STRIP = 2048
STRIPS = 2
MESH = pl.DeviceIdType.MESH


def transfer_rows(width, slots):
    tiles = -(-width // LANES)
    return -(-(tiles * slots) // 16) * 16


def iota(shape, axis):
    return lax.broadcasted_iota(jnp.int32, shape, axis)


def pack_strip(chosen, staging, width, slots):
    for start in range(0, width, LANES):
        tile = start // LANES
        stop = min(start + LANES, width)
        staging[:, slots * tile : slots * (tile + 1), 0 : stop - start] = chosen[
            :, 0:slots, start:stop
        ]


def unpack_strip(staging, spread, width, slots):
    for start in range(0, width, LANES):
        tile = start // LANES
        stop = min(start + LANES, width)
        spread[:, 0:slots, start:stop] = staging[
            :, slots * tile : slots * (tile + 1), 0 : stop - start
        ]


def merge_kernel(
    blocks,
    col_blocks,
    slots,
    window_ref,
    rest_ref,
    pairs_ref,
    count_ref,
    window_out,
    rest_out,
    send_main,
    got_main,
    send_tail,
    got_tail,
    send_win,
    got_win,
    mixed,
    staging,
    spread,
    place_ref,
    keep_ref,
    take_ref,
    load_sem,
    send_sem,
    recv_sem,
    col_send_sem,
    col_recv_sem,
):
    rows, window_cols = window_ref.shape
    cols = rest_ref.shape[1]
    pair_count = pairs_ref.shape[0]
    chunk = STRIP * STRIPS
    chunks = cols // chunk
    tail = cols - chunks * chunk
    strip_rows = slots * (STRIP // LANES)
    me = lax.axis_index("row")
    my_col = lax.axis_index("col")
    order = sorted(range(1, blocks), key=lambda m: (abs(m - blocks // 2), m))

    loads = [
        pltpu.make_async_copy(
            rest_ref.at[:, pl.ds(c * chunk, chunk)],
            rest_out.at[:, pl.ds(c * chunk, chunk)],
            load_sem.at[c],
        )
        for c in range(chunks)
    ]
    if tail:
        loads.append(
            pltpu.make_async_copy(
                rest_ref.at[:, pl.ds(chunks * chunk, tail)],
                rest_out.at[:, pl.ds(chunks * chunk, tail)],
                load_sem.at[chunks],
            )
        )
    for load in loads:
        load.start()

    barrier = pltpu.get_barrier_semaphore()
    for m in range(1, blocks):
        pl.semaphore_signal(
            barrier, inc=1, device_id=(lax.rem(me + m, blocks), my_col), device_id_type=MESH
        )
    for m in range(1, col_blocks):
        pl.semaphore_signal(
            barrier, inc=1, device_id=(me, lax.rem(my_col + m, col_blocks)), device_id_type=MESH
        )

    survivor_s = pairs_ref[:, 0:1]
    partner_s = pairs_ref[:, 1:2]
    square = (pair_count, pair_count)
    diagonal = iota(square, 0) == iota(square, 1)

    def along_lanes(column):
        return jnp.sum(jnp.where(diagonal, column, jnp.zeros_like(column)), axis=0, keepdims=True)

    def block_of(items):
        block = jnp.zeros_like(items)
        for b in range(1, blocks):
            block = block + (items >= b * rows).astype(jnp.int32)
        return block

    survivor_l = along_lanes(survivor_s)
    partner_l = along_lanes(partner_s)
    src_s, src_l = block_of(partner_s), block_of(partner_l)
    dst_s, dst_l = block_of(survivor_s), block_of(survivor_l)
    same = (src_s * blocks + dst_s) == (src_l * blocks + dst_l)
    rank_l = jnp.sum(
        jnp.where(same & (iota(square, 0) < iota(square, 1)), 1, 0), axis=0, keepdims=True
    )
    rank_s = jnp.sum(
        jnp.where(same & (iota(square, 1) < iota(square, 0)), 1, 0), axis=1, keepdims=True
    )
    slot_shape = (blocks * GROUP, pair_count)
    slot_hot = (iota(slot_shape, 0) == dst_l * GROUP + rank_l) & (src_l == me)
    row_hot = (partner_s - me * rows) == iota((pair_count, rows), 1)
    selector = jnp.dot(
        jnp.where(slot_hot, 1.0, 0.0).astype(jnp.bfloat16),
        jnp.where(row_hot, 1.0, 0.0).astype(jnp.bfloat16),
        preferred_element_type=jnp.float32,
    ).astype(jnp.bfloat16)

    staging[...] = jnp.zeros_like(staging)

    def choose(values, width):
        chosen = jnp.dot(selector, values, preferred_element_type=jnp.float32)
        pack_strip(chosen.reshape(blocks, GROUP, width), staging, width, slots)

    def row_copy(src, dst, index, peer, slot):
        return pltpu.make_async_remote_copy(
            src_ref=src,
            dst_ref=dst,
            send_sem=send_sem.at[index, peer],
            recv_sem=recv_sem.at[index, slot],
            device_id=(peer, my_col),
            device_id_type=MESH,
        )

    win_rows = send_win.shape[1]
    choose(window_ref[...], window_cols)
    send_win[...] = staging[:, 0:win_rows, :].astype(jnp.bfloat16)
    got_win[me] = send_win[me]
    pl.semaphore_wait(barrier, blocks - 1 + col_blocks - 1)
    for m in order:
        peer = lax.rem(me + m, blocks)
        row_copy(send_win.at[peer], got_win.at[me], chunks + 1, peer, me).start()

    def send_chunk(c, carry):
        pltpu.make_async_copy(
            rest_ref.at[:, pl.ds(0, chunk)], rest_out.at[:, pl.ds(0, chunk)], load_sem.at[c]
        ).wait()
        for j in range(STRIPS):
            first = pl.multiple_of(c * chunk + j * STRIP, LANES)
            choose(rest_out[:, pl.ds(first, STRIP)], STRIP)
            send_main[c, :, j * strip_rows : (j + 1) * strip_rows, :] = staging[
                :, 0:strip_rows, :
            ].astype(jnp.bfloat16)
        for m in order:
            peer = lax.rem(me + m, blocks)
            row_copy(send_main.at[c, peer], got_main.at[c, me], c, peer, me).start()
        got_main[c, me] = send_main[c, me]
        return carry

    lax.fori_loop(0, chunks, send_chunk, 0)

    tail_strips = [(s, min(STRIP, tail - s)) for s in range(0, tail, STRIP)]
    if tail:
        loads[chunks].wait()
        for start, width in tail_strips:
            choose(rest_out[:, chunks * chunk + start : chunks * chunk + start + width], width)
            at = slots * (start // LANES)
            size = transfer_rows(width, slots)
            send_tail[:, at : at + size, :] = staging[:, 0:size, :].astype(jnp.bfloat16)
        for m in order:
            peer = lax.rem(me + m, blocks)
            row_copy(send_tail.at[peer], got_tail.at[me], chunks, peer, me).start()
        got_tail[me] = send_tail[me]

    recv_hot = iota((pair_count, blocks * GROUP), 1) == src_s * GROUP + rank_s
    target_hot = (survivor_l - me * rows) == iota((rows, pair_count), 0)
    place_ref[...] = jnp.dot(
        jnp.where(target_hot, 1.0, 0.0).astype(jnp.bfloat16),
        jnp.where(recv_hot, 1.0, 0.0).astype(jnp.bfloat16),
        preferred_element_type=jnp.float32,
    ).astype(jnp.bfloat16)

    lanes_shape = (pair_count, LANES)

    def look_up(step, sums):
        kept, gone = sums
        first = pl.multiple_of(step * LANES, LANES)
        counts = count_ref[:, pl.ds(first, LANES)]
        item = iota(lanes_shape, 1) + step * LANES
        return (
            kept + jnp.where(item == survivor_s, counts, 0),
            gone + jnp.where(item == partner_s, counts, 0),
        )

    zeros = jnp.zeros(lanes_shape, jnp.int32)
    kept, gone = lax.fori_loop(0, count_ref.shape[1] // LANES, look_up, (zeros, zeros))
    kept = jnp.sum(kept, axis=1, keepdims=True).astype(jnp.float32)
    gone = jnp.sum(gone, axis=1, keepdims=True).astype(jnp.float32)
    retained_s = kept / (kept + gone)
    selected_s = gone / (kept + gone)
    retained_l, selected_l = along_lanes(retained_s), along_lanes(selected_s)

    item_rows = me * rows + iota((rows, pair_count), 0)
    survives = item_rows == survivor_l
    vanishes = item_rows == partner_l
    keep_ref[...] = jnp.broadcast_to(
        1.0
        - jnp.sum(jnp.where(survives | vanishes, 1.0, 0.0), axis=1, keepdims=True)
        + jnp.sum(jnp.where(survives, retained_l, 0.0), axis=1, keepdims=True),
        keep_ref.shape,
    )
    take_ref[...] = jnp.broadcast_to(
        jnp.sum(jnp.where(survives, selected_l, 0.0), axis=1, keepdims=True), take_ref.shape
    )
    item_cols = my_col * window_cols + iota((pair_count, window_cols), 1)
    survives = item_cols == survivor_s
    vanishes = item_cols == partner_s
    col_keep = (
        1.0
        - jnp.sum(jnp.where(survives | vanishes, 1.0, 0.0), axis=0, keepdims=True)
        + jnp.sum(jnp.where(survives, retained_s, 0.0), axis=0, keepdims=True)
    )
    col_take = jnp.sum(jnp.where(survives, selected_s, 0.0), axis=0, keepdims=True)
    col_source = jnp.sum(jnp.where(survives, partner_s, 0), axis=0, keepdims=True)

    spread[...] = jnp.zeros_like(spread)

    def mix(own, width):
        unpack_strip(staging, spread, width, slots)
        moved = spread[:, :, 0:width].reshape(blocks * GROUP, width).astype(jnp.bfloat16)
        placed = jnp.dot(place_ref[...], moved, preferred_element_type=jnp.float32)
        return (
            keep_ref[:, 0:1] * own.astype(jnp.float32) + take_ref[:, 0:1] * placed
        ).astype(jnp.bfloat16)

    for m in order:
        peer = lax.rem(me + m, blocks)
        row_copy(send_win.at[peer], got_win.at[peer], chunks + 1, peer, peer).wait_recv()
    staging[:, 0:win_rows, :] = got_win[...].astype(jnp.float32)
    mixed[my_col] = mix(window_ref[...], window_cols)

    def col_copy(source, peer):
        return pltpu.make_async_remote_copy(
            src_ref=mixed.at[my_col],
            dst_ref=mixed.at[source],
            send_sem=col_send_sem.at[peer],
            recv_sem=col_recv_sem.at[source],
            device_id=(me, peer),
            device_id_type=MESH,
        )

    for m in range(1, col_blocks):
        col_copy(my_col, lax.rem(my_col + m, col_blocks)).start()

    def mix_chunk(c, carry):
        for m in order:
            peer = lax.rem(me + m, blocks)
            row_copy(send_main.at[c, peer], got_main.at[c, peer], c, peer, peer).wait_recv()
        for j in range(STRIPS):
            first = pl.multiple_of(c * chunk + j * STRIP, LANES)
            staging[:, 0:strip_rows, :] = got_main[
                c, :, j * strip_rows : (j + 1) * strip_rows, :
            ].astype(jnp.float32)
            rest_out[:, pl.ds(first, STRIP)] = mix(rest_out[:, pl.ds(first, STRIP)], STRIP)
        return carry

    def finish_window():
        for m in range(1, col_blocks):
            peer = lax.rem(my_col + m, col_blocks)
            col_copy(peer, peer).wait_recv()

        def gather(b, total):
            picker = (iota((window_cols, window_cols), 0) + b * window_cols) == col_source
            return total + jnp.dot(
                mixed[b],
                jnp.where(picker, 1.0, 0.0).astype(jnp.bfloat16),
                preferred_element_type=jnp.float32,
            )

        gathered = lax.fori_loop(
            0, col_blocks, gather, jnp.zeros((rows, window_cols), jnp.float32)
        )
        window_out[...] = (
            col_keep * mixed[my_col].astype(jnp.float32) + col_take * gathered
        ).astype(jnp.bfloat16)

    half = chunks // 2
    lax.fori_loop(0, half, mix_chunk, 0)
    finish_window()
    lax.fori_loop(half, chunks, mix_chunk, 0)

    if tail:
        for m in order:
            peer = lax.rem(me + m, blocks)
            row_copy(send_tail.at[peer], got_tail.at[peer], chunks, peer, peer).wait_recv()
        for start, width in tail_strips:
            at = slots * (start // LANES)
            size = transfer_rows(width, slots)
            staging[:, 0:size, :] = got_tail[:, at : at + size, :].astype(jnp.float32)
            place = slice(chunks * chunk + start, chunks * chunk + start + width)
            rest_out[:, place] = mix(rest_out[:, place], width)

    def drain(c, carry):
        for m in order:
            peer = lax.rem(me + m, blocks)
            row_copy(send_main.at[c, peer], got_main.at[c, me], c, peer, me).wait_send()
        return carry

    lax.fori_loop(0, chunks, drain, 0)
    for m in order:
        peer = lax.rem(me + m, blocks)
        row_copy(send_win.at[peer], got_win.at[me], chunks + 1, peer, me).wait_send()
        if tail:
            row_copy(send_tail.at[peer], got_tail.at[me], chunks, peer, me).wait_send()
    for m in range(1, col_blocks):
        col_copy(my_col, lax.rem(my_col + m, col_blocks)).wait_send()


def shards(sim_window, sim_rest, joined_partner_pairs, cluster_member_count):
    blocks = lax.axis_size("row")
    col_blocks = lax.axis_size("col")
    rows, window_cols = sim_window.shape
    cols = sim_rest.shape[1]
    slots = rows // 64
    chunk = STRIP * STRIPS
    chunks = cols // chunk
    tail = cols - chunks * chunk
    main_rows = slots * (chunk // LANES)
    tail_rows = max(16, transfer_rows(tail, slots))
    win_rows = transfer_rows(window_cols, slots)
    stage_rows = max(slots * (STRIP // LANES), win_rows)
    bf16, f32 = jnp.bfloat16, jnp.float32
    vmem = pl.BlockSpec(memory_space=pltpu.VMEM)
    return pl.pallas_call(
        functools.partial(merge_kernel, blocks, col_blocks, slots),
        out_shape=(
            jax.ShapeDtypeStruct(sim_window.shape, bf16),
            jax.ShapeDtypeStruct(sim_rest.shape, bf16),
        ),
        in_specs=[vmem, pl.BlockSpec(memory_space=pl.ANY), vmem, vmem],
        out_specs=(vmem, vmem),
        scratch_shapes=[
            pltpu.VMEM((chunks, blocks, main_rows, LANES), bf16),
            pltpu.VMEM((chunks, blocks, main_rows, LANES), bf16),
            pltpu.VMEM((blocks, tail_rows, LANES), bf16),
            pltpu.VMEM((blocks, tail_rows, LANES), bf16),
            pltpu.VMEM((blocks, win_rows, LANES), bf16),
            pltpu.VMEM((blocks, win_rows, LANES), bf16),
            pltpu.VMEM((col_blocks, rows, window_cols), bf16),
            pltpu.VMEM((blocks, stage_rows, LANES), f32),
            pltpu.VMEM((blocks, GROUP, STRIP), f32),
            pltpu.VMEM((rows, blocks * GROUP), bf16),
            pltpu.VMEM((rows, LANES), f32),
            pltpu.VMEM((rows, LANES), f32),
            pltpu.SemaphoreType.DMA((chunks + 1,)),
            pltpu.SemaphoreType.DMA((chunks + 2, blocks)),
            pltpu.SemaphoreType.DMA((chunks + 2, blocks)),
            pltpu.SemaphoreType.DMA((col_blocks,)),
            pltpu.SemaphoreType.DMA((col_blocks,)),
        ],
        compiler_params=pltpu.CompilerParams(
            collective_id=0, has_side_effects=True, vmem_limit_bytes=44 * 1024 * 1024
        ),
        name="merge",
    )(sim_window, sim_rest, joined_partner_pairs, cluster_member_count.reshape(1, -1))


def solution(mesh):
    in_specs = (P("row", "col"), P("row", "col"), P(), P())
    out_specs = (P("row", "col"), P("row", "col"))
    return jax.shard_map(shards, mesh=mesh, in_specs=in_specs, out_specs=out_specs, check_vma=False)
```

```python
import functools

import jax
import jax.numpy as jnp
from jax import lax
from jax.experimental import pallas as pl
from jax.experimental.pallas import tpu as pltpu
from jax.sharding import PartitionSpec as P

LANES = 128
GROUP = 8
STRIP = 2048
STRIPS = 4
MESH = pl.DeviceIdType.MESH


def transfer_rows(width, slots):
    tiles = -(-width // LANES)
    return -(-(tiles * slots) // 16) * 16


def iota(shape, axis):
    return lax.broadcasted_iota(jnp.int32, shape, axis)


def pack_strip(chosen, staging, width, slots):
    for start in range(0, width, LANES):
        tile = start // LANES
        stop = min(start + LANES, width)
        staging[:, slots * tile : slots * (tile + 1), 0 : stop - start] = chosen[
            :, 0:slots, start:stop
        ]


def unpack_strip(staging, spread, width, slots):
    for start in range(0, width, LANES):
        tile = start // LANES
        stop = min(start + LANES, width)
        spread[:, 0:slots, start:stop] = staging[
            :, slots * tile : slots * (tile + 1), 0 : stop - start
        ]


def merge_kernel(
    blocks,
    col_blocks,
    slots,
    window_hbm,
    rest_ref,
    pairs_hbm,
    count_hbm,
    window_out,
    rest_out,
    send_main,
    got_main,
    send_tail,
    got_tail,
    send_win,
    got_win,
    window_ref,
    pairs_ref,
    count_line,
    count_ref,
    mixed,
    staging,
    spread,
    place_ref,
    keep_ref,
    take_ref,
    small_sem,
    load_sem,
    send_sem,
    recv_sem,
    col_send_sem,
    col_recv_sem,
):
    rows, window_cols = window_hbm.shape
    cols = rest_ref.shape[1]
    pair_count = pairs_hbm.shape[1]
    chunk = STRIP * STRIPS
    chunks = cols // chunk
    tail = cols - chunks * chunk
    strip_rows = slots * (STRIP // LANES)
    me = lax.axis_index("row")
    my_col = lax.axis_index("col")
    order = sorted(range(1, blocks), key=lambda m: (abs(m - blocks // 2), m))

    loads = [
        pltpu.make_async_copy(
            rest_ref.at[:, pl.ds(c * chunk, chunk)],
            rest_out.at[:, pl.ds(c * chunk, chunk)],
            load_sem.at[c],
        )
        for c in range(chunks)
    ]
    if tail:
        loads.append(
            pltpu.make_async_copy(
                rest_ref.at[:, pl.ds(chunks * chunk, tail)],
                rest_out.at[:, pl.ds(chunks * chunk, tail)],
                load_sem.at[chunks],
            )
        )
    small_loads = [
        pltpu.make_async_copy(pairs_hbm, pairs_ref, small_sem.at[0]),
        pltpu.make_async_copy(window_hbm, window_ref, small_sem.at[1]),
        pltpu.make_async_copy(count_hbm, count_line, small_sem.at[2]),
    ]
    for load in small_loads + loads:
        load.start()

    barrier = pltpu.get_barrier_semaphore()
    for m in range(1, blocks):
        pl.semaphore_signal(
            barrier, inc=1, device_id=(lax.rem(me + m, blocks), my_col), device_id_type=MESH
        )
    for m in range(1, col_blocks):
        pl.semaphore_signal(
            barrier, inc=1, device_id=(me, lax.rem(my_col + m, col_blocks)), device_id_type=MESH
        )

    small_loads[0].wait()
    survivor_l = pairs_ref[0:1, :]
    partner_l = pairs_ref[1:2, :]
    square = (pair_count, pair_count)
    diagonal = iota(square, 0) == iota(square, 1)

    def along_lanes(column):
        return jnp.sum(jnp.where(diagonal, column, jnp.zeros_like(column)), axis=0, keepdims=True)

    def down_sublanes(line):
        return jnp.sum(jnp.where(diagonal, line, jnp.zeros_like(line)), axis=1, keepdims=True)

    def block_of(items):
        block = jnp.zeros_like(items)
        for b in range(1, blocks):
            block = block + (items >= b * rows).astype(jnp.int32)
        return block

    survivor_s = down_sublanes(survivor_l)
    partner_s = down_sublanes(partner_l)
    src_s, src_l = block_of(partner_s), block_of(partner_l)
    dst_s, dst_l = block_of(survivor_s), block_of(survivor_l)
    same = (src_s * blocks + dst_s) == (src_l * blocks + dst_l)
    rank_l = jnp.sum(
        jnp.where(same & (iota(square, 0) < iota(square, 1)), 1, 0), axis=0, keepdims=True
    )
    rank_s = jnp.sum(
        jnp.where(same & (iota(square, 1) < iota(square, 0)), 1, 0), axis=1, keepdims=True
    )
    slot_shape = (blocks * GROUP, pair_count)
    slot_hot = (iota(slot_shape, 0) == dst_l * GROUP + rank_l) & (src_l == me)
    row_hot = (partner_s - me * rows) == iota((pair_count, rows), 1)
    selector = jnp.dot(
        jnp.where(slot_hot, 1.0, 0.0).astype(jnp.bfloat16),
        jnp.where(row_hot, 1.0, 0.0).astype(jnp.bfloat16),
        preferred_element_type=jnp.float32,
    ).astype(jnp.bfloat16)

    staging[...] = jnp.zeros_like(staging)

    def choose(values, width):
        chosen = jnp.dot(selector, values, preferred_element_type=jnp.float32)
        pack_strip(chosen.reshape(blocks, GROUP, width), staging, width, slots)

    def row_copy(src, dst, index, peer, slot):
        return pltpu.make_async_remote_copy(
            src_ref=src,
            dst_ref=dst,
            send_sem=send_sem.at[index, peer],
            recv_sem=recv_sem.at[index, slot],
            device_id=(peer, my_col),
            device_id_type=MESH,
        )

    small_loads[1].wait()
    win_rows = send_win.shape[1]
    choose(window_ref[...], window_cols)
    send_win[...] = staging[:, 0:win_rows, :].astype(jnp.bfloat16)
    got_win[me] = send_win[me]
    pl.semaphore_wait(barrier, blocks - 1 + col_blocks - 1)
    for m in order:
        peer = lax.rem(me + m, blocks)
        row_copy(send_win.at[peer], got_win.at[me], chunks + 1, peer, me).start()

    def send_chunk(c, carry):
        pltpu.make_async_copy(
            rest_ref.at[:, pl.ds(0, chunk)], rest_out.at[:, pl.ds(0, chunk)], load_sem.at[c]
        ).wait()
        for j in range(STRIPS):
            first = pl.multiple_of(c * chunk + j * STRIP, LANES)
            choose(rest_out[:, pl.ds(first, STRIP)], STRIP)
            send_main[c, :, j * strip_rows : (j + 1) * strip_rows, :] = staging[
                :, 0:strip_rows, :
            ].astype(jnp.bfloat16)
        for m in order:
            peer = lax.rem(me + m, blocks)
            row_copy(send_main.at[c, peer], got_main.at[c, me], c, peer, me).start()
        got_main[c, me] = send_main[c, me]
        return carry

    lax.fori_loop(0, chunks, send_chunk, 0)

    tail_strips = [(s, min(STRIP, tail - s)) for s in range(0, tail, STRIP)]
    if tail:
        loads[chunks].wait()
        for start, width in tail_strips:
            choose(rest_out[:, chunks * chunk + start : chunks * chunk + start + width], width)
            at = slots * (start // LANES)
            size = transfer_rows(width, slots)
            send_tail[:, at : at + size, :] = staging[:, 0:size, :].astype(jnp.bfloat16)
        for m in order:
            peer = lax.rem(me + m, blocks)
            row_copy(send_tail.at[peer], got_tail.at[me], chunks, peer, me).start()
        got_tail[me] = send_tail[me]

    recv_hot = iota((pair_count, blocks * GROUP), 1) == src_s * GROUP + rank_s
    target_hot = (survivor_l - me * rows) == iota((rows, pair_count), 0)
    place_ref[...] = jnp.dot(
        jnp.where(target_hot, 1.0, 0.0).astype(jnp.bfloat16),
        jnp.where(recv_hot, 1.0, 0.0).astype(jnp.bfloat16),
        preferred_element_type=jnp.float32,
    ).astype(jnp.bfloat16)

    small_loads[2].wait()
    count_ref[...] = count_line[...].reshape(count_ref.shape)
    lanes_shape = (pair_count, LANES)

    def look_up(step, sums):
        kept, gone = sums
        first = pl.multiple_of(step * LANES, LANES)
        counts = count_ref[:, pl.ds(first, LANES)]
        item = iota(lanes_shape, 1) + step * LANES
        return (
            kept + jnp.where(item == survivor_s, counts, 0),
            gone + jnp.where(item == partner_s, counts, 0),
        )

    zeros = jnp.zeros(lanes_shape, jnp.int32)
    kept, gone = lax.fori_loop(0, count_ref.shape[1] // LANES, look_up, (zeros, zeros))
    kept = jnp.sum(kept, axis=1, keepdims=True).astype(jnp.float32)
    gone = jnp.sum(gone, axis=1, keepdims=True).astype(jnp.float32)
    retained_s = kept / (kept + gone)
    selected_s = gone / (kept + gone)
    retained_l, selected_l = along_lanes(retained_s), along_lanes(selected_s)

    item_rows = me * rows + iota((rows, pair_count), 0)
    survives = item_rows == survivor_l
    vanishes = item_rows == partner_l
    keep_ref[...] = jnp.broadcast_to(
        1.0
        - jnp.sum(jnp.where(survives | vanishes, 1.0, 0.0), axis=1, keepdims=True)
        + jnp.sum(jnp.where(survives, retained_l, 0.0), axis=1, keepdims=True),
        keep_ref.shape,
    )
    take_ref[...] = jnp.broadcast_to(
        jnp.sum(jnp.where(survives, selected_l, 0.0), axis=1, keepdims=True), take_ref.shape
    )
    item_cols = my_col * window_cols + iota((pair_count, window_cols), 1)
    survives = item_cols == survivor_s
    vanishes = item_cols == partner_s
    col_keep = (
        1.0
        - jnp.sum(jnp.where(survives | vanishes, 1.0, 0.0), axis=0, keepdims=True)
        + jnp.sum(jnp.where(survives, retained_s, 0.0), axis=0, keepdims=True)
    )
    col_take = jnp.sum(jnp.where(survives, selected_s, 0.0), axis=0, keepdims=True)
    col_source = jnp.sum(jnp.where(survives, partner_s, 0), axis=0, keepdims=True)

    spread[...] = jnp.zeros_like(spread)

    def mix(own, width):
        unpack_strip(staging, spread, width, slots)
        moved = spread[:, :, 0:width].reshape(blocks * GROUP, width).astype(jnp.bfloat16)
        placed = jnp.dot(place_ref[...], moved, preferred_element_type=jnp.float32)
        return (
            keep_ref[:, 0:1] * own.astype(jnp.float32) + take_ref[:, 0:1] * placed
        ).astype(jnp.bfloat16)

    for m in order:
        peer = lax.rem(me + m, blocks)
        row_copy(send_win.at[peer], got_win.at[peer], chunks + 1, peer, peer).wait_recv()
    staging[:, 0:win_rows, :] = got_win[...].astype(jnp.float32)
    mixed[my_col] = mix(window_ref[...], window_cols)

    def col_copy(source, peer):
        return pltpu.make_async_remote_copy(
            src_ref=mixed.at[my_col],
            dst_ref=mixed.at[source],
            send_sem=col_send_sem.at[peer],
            recv_sem=col_recv_sem.at[source],
            device_id=(me, peer),
            device_id_type=MESH,
        )

    for m in range(1, col_blocks):
        col_copy(my_col, lax.rem(my_col + m, col_blocks)).start()

    def mix_chunk(c, carry):
        for m in order:
            peer = lax.rem(me + m, blocks)
            row_copy(send_main.at[c, peer], got_main.at[c, peer], c, peer, peer).wait_recv()
        for j in range(STRIPS):
            first = pl.multiple_of(c * chunk + j * STRIP, LANES)
            staging[:, 0:strip_rows, :] = got_main[
                c, :, j * strip_rows : (j + 1) * strip_rows, :
            ].astype(jnp.float32)
            rest_out[:, pl.ds(first, STRIP)] = mix(rest_out[:, pl.ds(first, STRIP)], STRIP)
        return carry

    def finish_window():
        for m in range(1, col_blocks):
            peer = lax.rem(my_col + m, col_blocks)
            col_copy(peer, peer).wait_recv()

        def gather(b, total):
            picker = (iota((window_cols, window_cols), 0) + b * window_cols) == col_source
            return total + jnp.dot(
                mixed[b],
                jnp.where(picker, 1.0, 0.0).astype(jnp.bfloat16),
                preferred_element_type=jnp.float32,
            )

        gathered = lax.fori_loop(
            0, col_blocks, gather, jnp.zeros((rows, window_cols), jnp.float32)
        )
        window_out[...] = (
            col_keep * mixed[my_col].astype(jnp.float32) + col_take * gathered
        ).astype(jnp.bfloat16)

    half = chunks // 2
    lax.fori_loop(0, half, mix_chunk, 0)
    finish_window()
    lax.fori_loop(half, chunks, mix_chunk, 0)

    if tail:
        for m in order:
            peer = lax.rem(me + m, blocks)
            row_copy(send_tail.at[peer], got_tail.at[peer], chunks, peer, peer).wait_recv()
        for start, width in tail_strips:
            at = slots * (start // LANES)
            size = transfer_rows(width, slots)
            staging[:, 0:size, :] = got_tail[:, at : at + size, :].astype(jnp.float32)
            place = slice(chunks * chunk + start, chunks * chunk + start + width)
            rest_out[:, place] = mix(rest_out[:, place], width)

    def drain(c, carry):
        for m in order:
            peer = lax.rem(me + m, blocks)
            row_copy(send_main.at[c, peer], got_main.at[c, me], c, peer, me).wait_send()
        return carry

    lax.fori_loop(0, chunks, drain, 0)
    for m in order:
        peer = lax.rem(me + m, blocks)
        row_copy(send_win.at[peer], got_win.at[me], chunks + 1, peer, me).wait_send()
        if tail:
            row_copy(send_tail.at[peer], got_tail.at[me], chunks, peer, me).wait_send()
    for m in range(1, col_blocks):
        col_copy(my_col, lax.rem(my_col + m, col_blocks)).wait_send()


def write_kernel(parts, window_ref, rest_ref, window_out, rest_out, sem):
    size = rest_ref.shape[0] // parts
    writes = [
        pltpu.make_async_copy(
            rest_ref.at[pl.ds(p * size, size)], rest_out.at[pl.ds(p * size, size)], sem.at[p]
        )
        for p in range(parts)
    ]
    writes.append(pltpu.make_async_copy(window_ref, window_out, sem.at[parts]))
    for write in writes:
        write.start()
    for write in writes:
        write.wait()


def shards(sim_window, sim_rest, joined_partner_pairs, cluster_member_count):
    blocks = lax.axis_size("row")
    col_blocks = lax.axis_size("col")
    rows, window_cols = sim_window.shape
    cols = sim_rest.shape[1]
    slots = rows // 64
    chunk = STRIP * STRIPS
    chunks = cols // chunk
    tail = cols - chunks * chunk
    main_rows = slots * (chunk // LANES)
    tail_rows = max(16, transfer_rows(tail, slots))
    win_rows = transfer_rows(window_cols, slots)
    stage_rows = max(slots * (STRIP // LANES), win_rows)
    bf16, f32 = jnp.bfloat16, jnp.float32
    vmem = pl.BlockSpec(memory_space=pltpu.VMEM)
    merged = pl.pallas_call(
        functools.partial(merge_kernel, blocks, col_blocks, slots),
        out_shape=(
            jax.ShapeDtypeStruct(sim_window.shape, bf16),
            jax.ShapeDtypeStruct(sim_rest.shape, bf16),
        ),
        in_specs=[pl.BlockSpec(memory_space=pltpu.HBM)] * 4,
        out_specs=(vmem, vmem),
        scratch_shapes=[
            pltpu.VMEM((chunks, blocks, main_rows, LANES), bf16),
            pltpu.VMEM((chunks, blocks, main_rows, LANES), bf16),
            pltpu.VMEM((blocks, tail_rows, LANES), bf16),
            pltpu.VMEM((blocks, tail_rows, LANES), bf16),
            pltpu.VMEM((blocks, win_rows, LANES), bf16),
            pltpu.VMEM((blocks, win_rows, LANES), bf16),
            pltpu.VMEM(sim_window.shape, bf16),
            pltpu.VMEM(joined_partner_pairs.shape[::-1], jnp.int32),
            pltpu.VMEM(cluster_member_count.shape, jnp.int32),
            pltpu.VMEM((1, cluster_member_count.shape[0]), jnp.int32),
            pltpu.VMEM((col_blocks, rows, window_cols), bf16),
            pltpu.VMEM((blocks, stage_rows, LANES), f32),
            pltpu.VMEM((blocks, GROUP, STRIP), f32),
            pltpu.VMEM((rows, blocks * GROUP), bf16),
            pltpu.VMEM((rows, LANES), f32),
            pltpu.VMEM((rows, LANES), f32),
            pltpu.SemaphoreType.DMA((3,)),
            pltpu.SemaphoreType.DMA((chunks + 1,)),
            pltpu.SemaphoreType.DMA((chunks + 2, blocks)),
            pltpu.SemaphoreType.DMA((chunks + 2, blocks)),
            pltpu.SemaphoreType.DMA((col_blocks,)),
            pltpu.SemaphoreType.DMA((col_blocks,)),
        ],
        compiler_params=pltpu.CompilerParams(
            collective_id=0, has_side_effects=True, vmem_limit_bytes=36 * 1024 * 1024
        ),
        name="merge",
    )(sim_window, sim_rest, joined_partner_pairs.T, cluster_member_count)
    hbm = pl.BlockSpec(memory_space=pltpu.HBM)
    parts = rows // 16
    return pl.pallas_call(
        functools.partial(write_kernel, parts),
        out_shape=(
            jax.ShapeDtypeStruct(sim_window.shape, bf16),
            jax.ShapeDtypeStruct(sim_rest.shape, bf16),
        ),
        in_specs=[vmem, vmem],
        out_specs=(hbm, hbm),
        scratch_shapes=[pltpu.SemaphoreType.DMA((parts + 1,))],
        compiler_params=pltpu.CompilerParams(vmem_limit_bytes=4 * 1024 * 1024),
        name="write",
    )(*merged)


def solution(mesh):
    in_specs = (P("row", "col"), P("row", "col"), P(), P())
    out_specs = (P("row", "col"), P("row", "col"))
    return jax.shard_map(shards, mesh=mesh, in_specs=in_specs, out_specs=out_specs, check_vma=False)
```

```python
import functools

import jax
import jax.numpy as jnp
from jax import lax
from jax.experimental import pallas as pl
from jax.experimental.pallas import tpu as pltpu
from jax.sharding import PartitionSpec as P

LANES = 128
GROUP = 8
STRIP = 2048
STRIPS = 4
MESH = pl.DeviceIdType.MESH


def transfer_rows(width, slots):
    tiles = -(-width // LANES)
    return -(-(tiles * slots) // 16) * 16


def iota(shape, axis):
    return lax.broadcasted_iota(jnp.int32, shape, axis)


def pack_strip(chosen, staging, width, slots):
    for start in range(0, width, LANES):
        tile = start // LANES
        stop = min(start + LANES, width)
        staging[:, slots * tile : slots * (tile + 1), 0 : stop - start] = chosen[
            :, 0:slots, start:stop
        ]


def unpack_strip(staging, spread, width, slots):
    for start in range(0, width, LANES):
        tile = start // LANES
        stop = min(start + LANES, width)
        spread[:, 0:slots, start:stop] = staging[
            :, slots * tile : slots * (tile + 1), 0 : stop - start
        ]


def merge_kernel(
    blocks,
    col_blocks,
    slots,
    window_hbm,
    rest_ref,
    pairs_hbm,
    count_hbm,
    window_out,
    rest_out,
    send_main,
    got_main,
    send_tail,
    got_tail,
    send_win,
    got_win,
    window_ref,
    pairs_ref,
    count_line,
    count_ref,
    mixed,
    staging,
    spread,
    place_ref,
    keep_ref,
    take_ref,
    small_sem,
    load_sem,
    send_sem,
    recv_sem,
    col_send_sem,
    col_recv_sem,
):
    rows, window_cols = window_hbm.shape
    cols = rest_ref.shape[1]
    pair_count = pairs_hbm.shape[1]
    chunk = STRIP * STRIPS
    chunks = cols // chunk
    tail = cols - chunks * chunk
    strip_rows = slots * (STRIP // LANES)
    me = lax.axis_index("row")
    my_col = lax.axis_index("col")
    order = sorted(range(1, blocks), key=lambda m: (abs(m - blocks // 2), m))

    loads = [
        pltpu.make_async_copy(
            rest_ref.at[:, pl.ds(c * chunk, chunk)],
            rest_out.at[:, pl.ds(c * chunk, chunk)],
            load_sem.at[c],
        )
        for c in range(chunks)
    ]
    if tail:
        loads.append(
            pltpu.make_async_copy(
                rest_ref.at[:, pl.ds(chunks * chunk, tail)],
                rest_out.at[:, pl.ds(chunks * chunk, tail)],
                load_sem.at[chunks],
            )
        )
    small_loads = [
        pltpu.make_async_copy(pairs_hbm, pairs_ref, small_sem.at[0]),
        pltpu.make_async_copy(window_hbm, window_ref, small_sem.at[1]),
        pltpu.make_async_copy(count_hbm, count_line, small_sem.at[2]),
    ]
    for load in small_loads + loads:
        load.start()

    barrier = pltpu.get_barrier_semaphore()
    for m in range(1, blocks):
        pl.semaphore_signal(
            barrier, inc=1, device_id=(lax.rem(me + m, blocks), my_col), device_id_type=MESH
        )
    for m in range(1, col_blocks):
        pl.semaphore_signal(
            barrier, inc=1, device_id=(me, lax.rem(my_col + m, col_blocks)), device_id_type=MESH
        )

    small_loads[0].wait()
    survivor_l = pairs_ref[0:1, :]
    partner_l = pairs_ref[1:2, :]
    square = (pair_count, pair_count)
    diagonal = iota(square, 0) == iota(square, 1)

    def along_lanes(column):
        return jnp.sum(jnp.where(diagonal, column, jnp.zeros_like(column)), axis=0, keepdims=True)

    def down_sublanes(line):
        return jnp.sum(jnp.where(diagonal, line, jnp.zeros_like(line)), axis=1, keepdims=True)

    def block_of(items):
        block = jnp.zeros_like(items)
        for b in range(1, blocks):
            block = block + (items >= b * rows).astype(jnp.int32)
        return block

    survivor_s = down_sublanes(survivor_l)
    partner_s = down_sublanes(partner_l)
    src_s, src_l = block_of(partner_s), block_of(partner_l)
    dst_s, dst_l = block_of(survivor_s), block_of(survivor_l)
    same = (src_s * blocks + dst_s) == (src_l * blocks + dst_l)
    rank_l = jnp.sum(
        jnp.where(same & (iota(square, 0) < iota(square, 1)), 1, 0), axis=0, keepdims=True
    )
    rank_s = jnp.sum(
        jnp.where(same & (iota(square, 1) < iota(square, 0)), 1, 0), axis=1, keepdims=True
    )
    slot_shape = (blocks * GROUP, pair_count)
    slot_hot = (iota(slot_shape, 0) == dst_l * GROUP + rank_l) & (src_l == me)
    row_hot = (partner_s - me * rows) == iota((pair_count, rows), 1)
    selector = jnp.dot(
        jnp.where(slot_hot, 1.0, 0.0).astype(jnp.bfloat16),
        jnp.where(row_hot, 1.0, 0.0).astype(jnp.bfloat16),
        preferred_element_type=jnp.float32,
    ).astype(jnp.bfloat16)

    staging[...] = jnp.zeros_like(staging)

    def choose(values, width):
        chosen = jnp.dot(selector, values, preferred_element_type=jnp.float32)
        pack_strip(chosen.reshape(blocks, GROUP, width), staging, width, slots)

    def row_copy(src, dst, index, peer, slot):
        return pltpu.make_async_remote_copy(
            src_ref=src,
            dst_ref=dst,
            send_sem=send_sem.at[index, peer],
            recv_sem=recv_sem.at[index, slot],
            device_id=(peer, my_col),
            device_id_type=MESH,
        )

    small_loads[1].wait()
    win_rows = send_win.shape[1]
    choose(window_ref[...], window_cols)
    send_win[...] = staging[:, 0:win_rows, :].astype(jnp.bfloat16)
    got_win[me] = send_win[me]
    pl.semaphore_wait(barrier, blocks - 1 + col_blocks - 1)
    for m in order:
        peer = lax.rem(me + m, blocks)
        row_copy(send_win.at[peer], got_win.at[me], chunks + 1, peer, me).start()

    def send_chunk(c, carry):
        pltpu.make_async_copy(
            rest_ref.at[:, pl.ds(0, chunk)], rest_out.at[:, pl.ds(0, chunk)], load_sem.at[c]
        ).wait()
        for j in range(STRIPS):
            first = pl.multiple_of(c * chunk + j * STRIP, LANES)
            choose(rest_out[:, pl.ds(first, STRIP)], STRIP)
            send_main[c, :, j * strip_rows : (j + 1) * strip_rows, :] = staging[
                :, 0:strip_rows, :
            ].astype(jnp.bfloat16)
        for m in order:
            peer = lax.rem(me + m, blocks)
            row_copy(send_main.at[c, peer], got_main.at[c, me], c, peer, me).start()
        got_main[c, me] = send_main[c, me]
        return carry

    lax.fori_loop(0, chunks, send_chunk, 0)

    tail_strips = [(s, min(STRIP, tail - s)) for s in range(0, tail, STRIP)]
    if tail:
        loads[chunks].wait()
        for start, width in tail_strips:
            choose(rest_out[:, chunks * chunk + start : chunks * chunk + start + width], width)
            at = slots * (start // LANES)
            size = transfer_rows(width, slots)
            send_tail[:, at : at + size, :] = staging[:, 0:size, :].astype(jnp.bfloat16)
        for m in order:
            peer = lax.rem(me + m, blocks)
            row_copy(send_tail.at[peer], got_tail.at[me], chunks, peer, me).start()
        got_tail[me] = send_tail[me]

    recv_hot = iota((pair_count, blocks * GROUP), 1) == src_s * GROUP + rank_s
    target_hot = (survivor_l - me * rows) == iota((rows, pair_count), 0)
    place_ref[...] = jnp.dot(
        jnp.where(target_hot, 1.0, 0.0).astype(jnp.bfloat16),
        jnp.where(recv_hot, 1.0, 0.0).astype(jnp.bfloat16),
        preferred_element_type=jnp.float32,
    ).astype(jnp.bfloat16)

    small_loads[2].wait()
    count_ref[...] = count_line[...].reshape(count_ref.shape)
    lanes_shape = (pair_count, LANES)

    def look_up(step, sums):
        kept, gone = sums
        first = pl.multiple_of(step * LANES, LANES)
        counts = count_ref[:, pl.ds(first, LANES)]
        item = iota(lanes_shape, 1) + step * LANES
        return (
            kept + jnp.where(item == survivor_s, counts, 0),
            gone + jnp.where(item == partner_s, counts, 0),
        )

    zeros = jnp.zeros(lanes_shape, jnp.int32)
    kept, gone = lax.fori_loop(0, count_ref.shape[1] // LANES, look_up, (zeros, zeros))
    kept = jnp.sum(kept, axis=1, keepdims=True).astype(jnp.float32)
    gone = jnp.sum(gone, axis=1, keepdims=True).astype(jnp.float32)
    retained_s = kept / (kept + gone)
    selected_s = gone / (kept + gone)
    retained_l, selected_l = along_lanes(retained_s), along_lanes(selected_s)

    item_rows = me * rows + iota((rows, pair_count), 0)
    survives = item_rows == survivor_l
    vanishes = item_rows == partner_l
    keep_ref[...] = jnp.broadcast_to(
        1.0
        - jnp.sum(jnp.where(survives | vanishes, 1.0, 0.0), axis=1, keepdims=True)
        + jnp.sum(jnp.where(survives, retained_l, 0.0), axis=1, keepdims=True),
        keep_ref.shape,
    )
    take_ref[...] = jnp.broadcast_to(
        jnp.sum(jnp.where(survives, selected_l, 0.0), axis=1, keepdims=True), take_ref.shape
    )
    item_cols = my_col * window_cols + iota((pair_count, window_cols), 1)
    survives = item_cols == survivor_s
    vanishes = item_cols == partner_s
    col_keep = (
        1.0
        - jnp.sum(jnp.where(survives | vanishes, 1.0, 0.0), axis=0, keepdims=True)
        + jnp.sum(jnp.where(survives, retained_s, 0.0), axis=0, keepdims=True)
    )
    col_take = jnp.sum(jnp.where(survives, selected_s, 0.0), axis=0, keepdims=True)
    col_source = jnp.sum(jnp.where(survives, partner_s, 0), axis=0, keepdims=True)

    spread[...] = jnp.zeros_like(spread)

    def mix(own, width):
        unpack_strip(staging, spread, width, slots)
        moved = spread[:, :, 0:width].reshape(blocks * GROUP, width).astype(jnp.bfloat16)
        placed = jnp.dot(place_ref[...], moved, preferred_element_type=jnp.float32)
        return (
            keep_ref[:, 0:1] * own.astype(jnp.float32) + take_ref[:, 0:1] * placed
        ).astype(jnp.bfloat16)

    for m in order:
        peer = lax.rem(me + m, blocks)
        row_copy(send_win.at[peer], got_win.at[peer], chunks + 1, peer, peer).wait_recv()
    staging[:, 0:win_rows, :] = got_win[...].astype(jnp.float32)
    mixed[my_col] = mix(window_ref[...], window_cols)

    def col_copy(source, peer):
        return pltpu.make_async_remote_copy(
            src_ref=mixed.at[my_col],
            dst_ref=mixed.at[source],
            send_sem=col_send_sem.at[peer],
            recv_sem=col_recv_sem.at[source],
            device_id=(me, peer),
            device_id_type=MESH,
        )

    for m in range(1, col_blocks):
        col_copy(my_col, lax.rem(my_col + m, col_blocks)).start()

    def mix_chunk(c, carry):
        for m in order:
            peer = lax.rem(me + m, blocks)
            row_copy(send_main.at[c, peer], got_main.at[c, peer], c, peer, peer).wait_recv()
        for j in range(STRIPS):
            first = pl.multiple_of(c * chunk + j * STRIP, LANES)
            staging[:, 0:strip_rows, :] = got_main[
                c, :, j * strip_rows : (j + 1) * strip_rows, :
            ].astype(jnp.float32)
            rest_out[:, pl.ds(first, STRIP)] = mix(rest_out[:, pl.ds(first, STRIP)], STRIP)
        return carry

    def finish_window():
        for m in range(1, col_blocks):
            peer = lax.rem(my_col + m, col_blocks)
            col_copy(peer, peer).wait_recv()

        def gather(b, total):
            picker = (iota((window_cols, window_cols), 0) + b * window_cols) == col_source
            return total + jnp.dot(
                mixed[b],
                jnp.where(picker, 1.0, 0.0).astype(jnp.bfloat16),
                preferred_element_type=jnp.float32,
            )

        gathered = lax.fori_loop(
            0, col_blocks, gather, jnp.zeros((rows, window_cols), jnp.float32)
        )
        window_out[...] = (
            col_keep * mixed[my_col].astype(jnp.float32) + col_take * gathered
        ).astype(jnp.bfloat16)

    half = chunks // 2
    lax.fori_loop(0, half, mix_chunk, 0)
    finish_window()
    lax.fori_loop(half, chunks, mix_chunk, 0)

    if tail:
        for m in order:
            peer = lax.rem(me + m, blocks)
            row_copy(send_tail.at[peer], got_tail.at[peer], chunks, peer, peer).wait_recv()
        for start, width in tail_strips:
            at = slots * (start // LANES)
            size = transfer_rows(width, slots)
            staging[:, 0:size, :] = got_tail[:, at : at + size, :].astype(jnp.float32)
            place = slice(chunks * chunk + start, chunks * chunk + start + width)
            rest_out[:, place] = mix(rest_out[:, place], width)

    def drain(c, carry):
        for m in order:
            peer = lax.rem(me + m, blocks)
            row_copy(send_main.at[c, peer], got_main.at[c, me], c, peer, me).wait_send()
        return carry

    lax.fori_loop(0, chunks, drain, 0)
    for m in order:
        peer = lax.rem(me + m, blocks)
        row_copy(send_win.at[peer], got_win.at[me], chunks + 1, peer, me).wait_send()
        if tail:
            row_copy(send_tail.at[peer], got_tail.at[me], chunks, peer, me).wait_send()
    for m in range(1, col_blocks):
        col_copy(my_col, lax.rem(my_col + m, col_blocks)).wait_send()


def write_kernel(parts, window_ref, rest_ref, window_out, rest_out, sem):
    size = rest_ref.shape[0] // parts
    writes = [
        pltpu.make_async_copy(
            rest_ref.at[pl.ds(p * size, size)], rest_out.at[pl.ds(p * size, size)], sem.at[p]
        )
        for p in range(parts)
    ]
    writes.append(pltpu.make_async_copy(window_ref, window_out, sem.at[parts]))
    for write in writes:
        write.start()
    for write in writes:
        write.wait()


def shards(sim_window, sim_rest, joined_partner_pairs, cluster_member_count):
    blocks = lax.axis_size("row")
    col_blocks = lax.axis_size("col")
    rows, window_cols = sim_window.shape
    cols = sim_rest.shape[1]
    slots = rows // 64
    chunk = STRIP * STRIPS
    chunks = cols // chunk
    tail = cols - chunks * chunk
    main_rows = slots * (chunk // LANES)
    tail_rows = max(16, transfer_rows(tail, slots))
    win_rows = transfer_rows(window_cols, slots)
    stage_rows = max(slots * (STRIP // LANES), win_rows)
    bf16, f32 = jnp.bfloat16, jnp.float32
    vmem = pl.BlockSpec(memory_space=pltpu.VMEM)
    merged = pl.pallas_call(
        functools.partial(merge_kernel, blocks, col_blocks, slots),
        out_shape=(
            jax.ShapeDtypeStruct(sim_window.shape, bf16),
            jax.ShapeDtypeStruct(sim_rest.shape, bf16),
        ),
        in_specs=[pl.BlockSpec(memory_space=pltpu.HBM)] * 4,
        out_specs=(vmem, vmem),
        scratch_shapes=[
            pltpu.VMEM((chunks, blocks, main_rows, LANES), bf16),
            pltpu.VMEM((chunks, blocks, main_rows, LANES), bf16),
            pltpu.VMEM((blocks, tail_rows, LANES), bf16),
            pltpu.VMEM((blocks, tail_rows, LANES), bf16),
            pltpu.VMEM((blocks, win_rows, LANES), bf16),
            pltpu.VMEM((blocks, win_rows, LANES), bf16),
            pltpu.VMEM(sim_window.shape, bf16),
            pltpu.VMEM(joined_partner_pairs.shape[::-1], jnp.int32),
            pltpu.VMEM(cluster_member_count.shape, jnp.int32),
            pltpu.VMEM((1, cluster_member_count.shape[0]), jnp.int32),
            pltpu.VMEM((col_blocks, rows, window_cols), bf16),
            pltpu.VMEM((blocks, stage_rows, LANES), f32),
            pltpu.VMEM((blocks, GROUP, STRIP), f32),
            pltpu.VMEM((rows, blocks * GROUP), bf16),
            pltpu.VMEM((rows, LANES), f32),
            pltpu.VMEM((rows, LANES), f32),
            pltpu.SemaphoreType.DMA((3,)),
            pltpu.SemaphoreType.DMA((chunks + 1,)),
            pltpu.SemaphoreType.DMA((chunks + 2, blocks)),
            pltpu.SemaphoreType.DMA((chunks + 2, blocks)),
            pltpu.SemaphoreType.DMA((col_blocks,)),
            pltpu.SemaphoreType.DMA((col_blocks,)),
        ],
        compiler_params=pltpu.CompilerParams(
            collective_id=0, has_side_effects=True, vmem_limit_bytes=36 * 1024 * 1024
        ),
        name="merge",
    )(
        pltpu.with_memory_space_constraint(sim_window, pltpu.HBM),
        sim_rest,
        pltpu.with_memory_space_constraint(joined_partner_pairs.T, pltpu.HBM),
        pltpu.with_memory_space_constraint(cluster_member_count, pltpu.HBM),
    )
    hbm = pl.BlockSpec(memory_space=pltpu.HBM)
    parts = rows // 16
    return pl.pallas_call(
        functools.partial(write_kernel, parts),
        out_shape=(
            jax.ShapeDtypeStruct(sim_window.shape, bf16),
            jax.ShapeDtypeStruct(sim_rest.shape, bf16),
        ),
        in_specs=[vmem, vmem],
        out_specs=(hbm, hbm),
        scratch_shapes=[pltpu.SemaphoreType.DMA((parts + 1,))],
        compiler_params=pltpu.CompilerParams(vmem_limit_bytes=4 * 1024 * 1024),
        name="write",
    )(*merged)


def solution(mesh):
    in_specs = (P("row", "col"), P("row", "col"), P(), P())
    out_specs = (P("row", "col"), P("row", "col"))
    return jax.shard_map(shards, mesh=mesh, in_specs=in_specs, out_specs=out_specs, check_vma=False)
```
